32 devices in a mesh: track: 16 (over z, x, core), ses: 2 (over y).
Axes of the slice: x: 2, y: 2, z: 4, core: 2. Of those that a mesh axis runs over, the one named last changes fastest.
Arguments:
- jacobians: float32 [2, 9, 8, 8192], P(None, None, None, ('track', 'ses')), may hold values from -6 to 6
- direction: float32 [6, 131072], P(None, ('track', 'ses')), may hold values from -50 to 50
- residual: float32 [6, 131072], P(None, ('track', 'ses')), may hold values from -50 to 50
- solution: float32 [6, 131072], P(None, ('track', 'ses')), may hold values from -6 to 6
- cam_damping: float32 [6, 131072], P(None, ('track', 'ses')), may hold values from 0.5 to 4
- precond: float32 [6, 6, 131072], P(None, None, ('track', 'ses')), may hold values from -0.15 to 2, as said below
- land_damping: float32 [8192], P(('track', 'ses')), may hold values from 0.5 to 4
- obs_slot: int32 [8, 8192], P(None, ('track', 'ses')), may hold values from 0 to 511, as said below
- obs_mask: int32 [8, 8192], P(None, ('track', 'ses')), may hold values from 0 to 1, as said below
- serve_rows: int32 [32, 512], P(('track', 'ses')), may hold values from 0 to 4095, as said below
Outputs:
- solution_new: float32 [6, 131072], P(None, ('track', 'ses'))
- residual_new: float32 [6, 131072], P(None, ('track', 'ses'))
- direction_new: float32 [6, 131072], P(None, ('track', 'ses'))
The draws below stay inside these ranges and needn't reach their ends.
Inputs may be any that keep to these rules, and one draw needn't show every extreme that they name: `obs_slot`: each slot names one keyframe that device s // 16 serves to the observing device; most slots name an owner in the observing device's own session block, the rest name owners anywhere. `serve_rows`: each row block of 16 entries lists distinct local keyframe rows of the owner. `obs_mask`: A track's live observation slots come first; every track has 2 to 8. `precond`: Symmetric, with a dominant positive diagonal.
All inputs are finite; a program needn't handle non-finite values.
Results may differ from the reference program's by a relative error of at most 0.0003.
Values sent between devices are 32-bit elements; how exact they have to be, the bound alone decides.
No kernel may reach another device: no remote copies, remote signals or barrier semaphores. Data moves between devices by JAX's collectives and lax.ppermute only.
A program may use at most 64 MiB of HBM per device.

```python
import math
import jax
import jax.numpy as jnp

TRK_DEV = 256
KF_DEV = 4096
CAP = 16
TRACKS = 8192
KF = 131072
N_TRACK = 16
N_SES = 2
DEVICES = 32


def rising_field(key):
    k_base, k_rough = jax.random.split(key)
    position = jnp.arange(KF, dtype=jnp.float32) / KF
    roughness = jnp.exp(jax.random.uniform(k_rough, (1, KF), minval=-1.15, maxval=1.15))
    base_draw = jax.random.truncated_normal(k_base, -4.0, 4.0, (6, KF))
    growth = jnp.exp(1.1 * position)
    return (base_draw * growth[None] * roughness).astype(jnp.float32)


def draw_direction(key, part):
    return rising_field(jax.random.fold_in(key, 11))


def draw_residual(key, part):
    return rising_field(jax.random.fold_in(key, 23))


def draw_precond(key, part):
    k_off, k_diag = jax.random.split(jax.random.fold_in(key, 37))
    raw_off = jax.random.uniform(k_off, (6, 6, KF), minval=-0.075, maxval=0.075)
    symmetric = raw_off + jnp.swapaxes(raw_off, 0, 1)
    identity_mat = (jnp.arange(6)[:, None] == jnp.arange(6)[None, :]).astype(jnp.float32)[:, :, None]
    diagonal = jnp.exp(jax.random.uniform(k_diag, (6, KF), minval=0.0, maxval=0.693))
    return (symmetric * (1.0 - identity_mat) + identity_mat * diagonal[None]).astype(jnp.float32)


def draw_obs_mask(key, part):
    lengths = jax.random.randint(jax.random.fold_in(key, 41), (1, TRACKS), 2, 9)
    return (jnp.arange(8, dtype=jnp.int32)[:, None] < lengths).astype(jnp.int32)


def draw_obs_slot(key, part):
    k_pick, k_near, k_far, k_within = jax.random.split(jax.random.fold_in(key, 61), 4)
    observer = jnp.arange(TRACKS, dtype=jnp.int32)[None, :] // TRK_DEV
    own_session = observer % N_SES
    near_owner = jax.random.randint(k_near, (8, TRACKS), 0, N_TRACK) * N_SES + own_session
    far_owner = jax.random.randint(k_far, (8, TRACKS), 0, DEVICES)
    pick = jax.random.randint(k_pick, (8, TRACKS), 0, 100)
    owner = jnp.where(pick < 85, near_owner, far_owner)
    slots = owner * CAP + jax.random.randint(k_within, (8, TRACKS), 0, CAP)
    flat = jnp.arange(8 * TRACKS, dtype=jnp.int32).reshape(8, TRACKS)
    slots = jnp.where(flat == 0, 0, slots)
    slots = jnp.where(flat == 8 * TRACKS - 1, DEVICES * CAP - 1, slots)
    return slots.astype(jnp.int32)


def draw_serve_rows(key, part):
    k_off, k_start = jax.random.split(jax.random.fold_in(key, 53))
    stride = KF_DEV // CAP
    offsets = jax.random.randint(k_off, (DEVICES, DEVICES, CAP), 0, stride)
    start_row = jax.random.randint(k_start, (DEVICES, DEVICES, 1), 0, KF_DEV)
    row_ids = (jnp.arange(CAP, dtype=jnp.int32)[None, None, :] * stride + offsets + start_row) % KF_DEV
    return row_ids.reshape(DEVICES, DEVICES * CAP).astype(jnp.int32)


def shard_levels(key, shape, pieces, least, high):
    def one(dim, parts):
        draws = jax.random.uniform(jax.random.fold_in(jax.random.fold_in(key, 6), dim), (parts,), jnp.float32, least / len(pieces), high / len(pieces))
        return jnp.repeat(jnp.exp(draws), shape[dim] // parts).reshape((-1,) + (1,) * (len(shape) - dim - 1))

    loudness = one(*pieces[0])
    for cut in pieces[1:]:
        loudness = loudness * one(*cut)
    return loudness


def normal_values(key, shape, deviation, bound, pieces=(), kind=jnp.bfloat16):
    factor_of = shard_levels(key, shape, pieces, -0.22, 0.18) if pieces else 1.0
    array = jax.random.normal(key, shape, jnp.float32) * deviation * factor_of
    return jnp.minimum(jnp.maximum(array, -bound), bound).astype(kind)


def setup_inputs(seed: int = 0) -> dict:
    key_of = jax.random.split(jax.random.key(seed), 11)
    return {
        "jacobians": normal_values(key_of[0], (2, 9, 8, TRACKS), 1.0, 6.0, ((3, 32),), jnp.float32),
        "direction": draw_direction(jax.random.fold_in(key_of[10], 71), 0),
        "residual": draw_residual(jax.random.fold_in(key_of[10], 71), 0),
        "solution": normal_values(key_of[3], (6, KF), 1.0, 6.0, ((1, 32),), jnp.float32),
        "cam_damping": jnp.clip(jnp.exp(math.log(4.0) - 2.0794415 * jax.random.uniform(key_of[4], (6, KF), jnp.float32) ** shard_levels(key_of[4], (6, KF), ((1, 32),), -0.2, 0.2)), 0.5, 4.0),
        "precond": draw_precond(jax.random.fold_in(key_of[10], 71), 0),
        "land_damping": jnp.clip(jnp.exp(math.log(4.0) - 2.0794415 * jax.random.uniform(key_of[6], (TRACKS,), jnp.float32) ** shard_levels(key_of[6], (TRACKS,), ((0, 32),), -0.2, 0.2)), 0.5, 4.0),
        "obs_slot": draw_obs_slot(jax.random.fold_in(key_of[10], 71), 0),
        "obs_mask": draw_obs_mask(jax.random.fold_in(key_of[10], 71), 0),
        "serve_rows": draw_serve_rows(jax.random.fold_in(key_of[10], 71), 0),
    }


def invert_three(matrix):
    cofactor = [[matrix[(i + 1) % 3, (j + 1) % 3] * matrix[(i + 2) % 3, (j + 2) % 3]
                 - matrix[(i + 1) % 3, (j + 2) % 3] * matrix[(i + 2) % 3, (j + 1) % 3]
                 for j in range(3)] for i in range(3)]
    determinant = matrix[0, 0] * cofactor[0][0] + matrix[0, 1] * cofactor[0][1] + matrix[0, 2] * cofactor[0][2]
    adjugate = jnp.stack([jnp.stack([cofactor[j][i] for j in range(3)]) for i in range(3)])
    return adjugate / determinant[None, None]


def track_terms(jacobian, camera_rows, live_mask, land_damp):
    cam_jac = jacobian[:, 0:6]
    land_jac = jacobian[:, 6:9]
    projected = jnp.sum(cam_jac * camera_rows[None], axis=1)
    weighted = land_jac * live_mask[None, None]
    normal_mat = jnp.sum(weighted[:, :, None] * land_jac[:, None, :], axis=(0, 3))
    identity_mat = (jnp.arange(3)[:, None] == jnp.arange(3)[None, :]).astype(jnp.float32)
    normal_mat = normal_mat + identity_mat[:, :, None] * land_damp[None, None]
    inverse = invert_three(normal_mat)
    landmark_rhs = jnp.sum(weighted * projected[:, None], axis=(0, 2))
    landmark_step = jnp.sum(inverse * landmark_rhs[None], axis=1)
    back_proj = jnp.sum(land_jac * landmark_step[None, :, None], axis=1)
    obs_res = live_mask[None] * (projected - back_proj)
    return jnp.sum(cam_jac * obs_res[:, None], axis=0)


def apply_precond(precond, vector):
    return jnp.sum(precond * vector[None], axis=1)


def reference(jacobians, direction, residual, solution, cam_damping, precond, land_damping, obs_slot, obs_mask, serve_rows):
    device_index = (jnp.arange(TRACKS, dtype=jnp.int32) // TRK_DEV)[None, :]
    source = obs_slot // CAP
    within = obs_slot % CAP
    local_row = serve_rows[source, device_index * CAP + within]
    keyframe = (source * KF_DEV + local_row).astype(jnp.int32)
    camera_rows = direction[:, keyframe]
    live_mask = obs_mask.astype(jnp.float32)
    gradient = track_terms(jacobians, camera_rows, live_mask, land_damping)
    summed = jnp.zeros((6, KF), jnp.float32).at[:, keyframe.reshape(-1)].add(gradient.reshape(6, -1))
    schur_image = cam_damping * direction + summed
    old_norm = jnp.sum(residual * apply_precond(precond, residual))
    curvature = jnp.sum(direction * schur_image)
    step_size = old_norm / curvature
    solution_new = solution + step_size * direction
    residual_new = residual - step_size * schur_image
    precond_res = apply_precond(precond, residual_new)
    new_norm = jnp.sum(residual_new * precond_res)
    direction_new = precond_res + (new_norm / old_norm) * direction
    return solution_new, residual_new, direction_new
```

```python
import functools

import jax
import jax.numpy as jnp
from jax import lax
from jax.experimental import pallas as pl
from jax.experimental.pallas import tpu as pltpu
from jax.sharding import PartitionSpec as P

LANES = 128
SUBS = 8
AXES = ("track", "ses")


def lane_gather(rows, index):
    return jnp.take_along_axis(rows, index, axis=1, mode="promise_in_bounds")


def spread(row, subs=SUBS):
    return jnp.broadcast_to(row, (subs, row.shape[1]))


def iota(shape, dim):
    return lax.broadcasted_iota(jnp.int32, shape, dim)


def each(count, body):
    if count <= 8:
        for j in range(count):
            body(j)
    else:
        lax.fori_loop(0, count, lambda j, c: (body(j), c)[1], 0)


def at_group(j):
    if isinstance(j, int):
        return pl.ds(j * LANES, LANES)
    return pl.ds(pl.multiple_of(j * LANES, LANES), LANES)


def at_rows(j, size=SUBS):
    if isinstance(j, int):
        return pl.ds(j * size, size)
    return pl.ds(pl.multiple_of(j * size, size), size)


def rows_to_blocks(rows, cap, params):
    per = LANES // cap
    lane = iota((per, LANES), 1)
    index = iota((per, LANES), 0) * cap + lane % cap
    out = jnp.zeros((per, LANES), rows.dtype)
    for k in range(params):
        picked = lane_gather(spread(rows[k : k + 1], per), index)
        out = jnp.where(lane // cap == k, picked, out)
    return out


def blocks_to_rows(blocks, cap, params):
    per = LANES // cap
    lane = iota((SUBS, LANES), 1)
    sub = iota((SUBS, LANES), 0)
    index = jnp.minimum(sub, params - 1) * cap + lane % cap
    out = jnp.zeros((SUBS, LANES), blocks.dtype)
    for src in range(per):
        picked = lane_gather(spread(blocks[src : src + 1]), index)
        out = jnp.where(lane // cap == src, picked, out)
    return jnp.where(sub < params, out, 0.0)


def split_bf16(value, parts):
    pieces = []
    rest = value
    for p in range(parts):
        piece = rest.astype(jnp.bfloat16)
        pieces.append(piece)
        if p + 1 < parts:
            rest = rest - piece.astype(jnp.float32)
    return pieces


def apply_precond(precond, vector):
    params = vector.shape[0]
    total = precond[0] * vector[0:1]
    for k in range(1, params):
        total = total + precond[k] * vector[k : k + 1]
    return total


def serve_kernel(cap, direction, served, outgoing):
    params, count = direction.shape
    groups = served.shape[1] // LANES
    per = LANES // cap

    def body(j):
        row = served[:, at_group(j)]
        low = spread(row % LANES, params)
        high = spread(row // LANES, params)
        rows = jnp.zeros((params, LANES), jnp.float32)
        for h in range(count // LANES):
            picked = lane_gather(direction[:, h * LANES : (h + 1) * LANES], low)
            rows = jnp.where(high == h, picked, rows)
        outgoing[at_rows(j, per), :] = rows_to_blocks(rows, cap, params)

    each(groups, body)


def norms_kernel(direction, residual, damping, precond, norms):
    params, count = direction.shape
    old = jnp.zeros((params, LANES), jnp.float32)
    curv = jnp.zeros((params, LANES), jnp.float32)
    for h in range(count // LANES):
        at = slice(h * LANES, (h + 1) * LANES)
        res = residual[:, at]
        pre = apply_precond([precond[k, :, at] for k in range(params)], res)
        old = old + res * pre
        dire = direction[:, at]
        curv = curv + damping[:, at] * dire * dire
    row = iota((SUBS, LANES), 0)
    norms[...] = jnp.where(row == 0, jnp.sum(old), jnp.where(row == 1, jnp.sum(curv), 0.0))


def track_kernel(cap, params, incoming, jac, slots, mask, damp, norms, returned, table):
    devices = incoming.shape[0]
    per = LANES // cap
    groups = devices // per
    obs, tracks = slots.shape

    def fill(j):
        table[:, at_group(j)] = blocks_to_rows(incoming[at_rows(j, per), :], cap, params)

    each(groups, fill)

    slot = slots[...]
    owner = slot // cap
    within = slot % cap
    halves = [slice(t * LANES, (t + 1) * LANES) for t in range(tracks // LANES)]
    low = [slot[:, at] % LANES for at in halves]
    high = [slot[:, at] // LANES for at in halves]

    def look(j, camera):
        rows = table[:, at_group(j)]
        out = []
        for k in range(params):
            source = spread(rows[k : k + 1], obs)
            for t in range(len(halves)):
                picked = lane_gather(source, low[t])
                out.append(jnp.where(high[t] == j, picked, camera[len(out)]))
        return tuple(out)

    camera = tuple(jnp.zeros((obs, LANES), jnp.float32) for _ in range(params * len(halves)))
    if groups <= 8:
        for j in range(groups):
            camera = look(j, camera)
    else:
        camera = lax.fori_loop(0, groups, look, camera)
    camera = [
        jnp.concatenate(camera[k * len(halves) : (k + 1) * len(halves)], axis=1)
        for k in range(params)
    ]

    live = mask[...].astype(jnp.float32)
    cam = [[jac[a, k] for k in range(params)] for a in range(2)]
    land = [[jac[a, params + i] for i in range(3)] for a in range(2)]
    projected = []
    for a in range(2):
        total = cam[a][0] * camera[0]
        for k in range(1, params):
            total = total + cam[a][k] * camera[k]
        projected.append(total)
    weighted = [[land[a][i] * live for i in range(3)] for a in range(2)]

    def over_slots(value):
        return jnp.sum(value, axis=0, keepdims=True)

    normal = {}
    for i in range(3):
        for j in range(i, 3):
            entry = over_slots(weighted[0][i] * land[0][j] + weighted[1][i] * land[1][j])
            if i == j:
                entry = entry + damp[...]
            normal[i, j] = entry
            normal[j, i] = entry
    rhs = [over_slots(weighted[0][i] * projected[0] + weighted[1][i] * projected[1]) for i in range(3)]
    cof = [
        [
            normal[(i + 1) % 3, (j + 1) % 3] * normal[(i + 2) % 3, (j + 2) % 3]
            - normal[(i + 1) % 3, (j + 2) % 3] * normal[(i + 2) % 3, (j + 1) % 3]
            for j in range(3)
        ]
        for i in range(3)
    ]
    det = normal[0, 0] * cof[0][0] + normal[0, 1] * cof[0][1] + normal[0, 2] * cof[0][2]
    step = [
        (cof[0][i] * rhs[0] + cof[1][i] * rhs[1] + cof[2][i] * rhs[2]) / det for i in range(3)
    ]
    res = [
        live
        * (projected[a] - (land[a][0] * step[0] + land[a][1] * step[1] + land[a][2] * step[2]))
        for a in range(2)
    ]
    curv = jnp.sum(res[0] * projected[0] + res[1] * projected[1])
    grad = [cam[0][k] * res[0] + cam[1][k] * res[1] for k in range(params)]

    owner_id = iota((devices, tracks), 0)
    within_id = iota((cap, tracks), 0)
    total = jnp.zeros((devices, LANES), jnp.float32)
    pad = LANES - params * cap
    for o in range(obs):
        at_owner = (spread(owner[o : o + 1], devices) == owner_id).astype(jnp.float32).astype(jnp.bfloat16)
        at_within = spread(within[o : o + 1], cap) == within_id
        values = [jnp.where(at_within, spread(grad[k][o : o + 1], cap), 0.0) for k in range(params)]
        if pad:
            values.append(jnp.zeros((pad, tracks), jnp.float32))
        values = jnp.concatenate(values, axis=0)
        for piece in split_bf16(values, 3):
            total = total + lax.dot_general(
                at_owner, piece, (((1,), (1,)), ((), ())), preferred_element_type=jnp.float32
            )
    lane = iota((devices, LANES), 1)
    old_part = spread(norms[0:1, :], devices)
    curv_part = spread(norms[1:2, :], devices) + curv
    total = jnp.where(lane == params * cap, old_part, total)
    returned[...] = jnp.where(lane == params * cap + 1, curv_part, total)


def owner_kernel(
    cap, arrived, served, direction, residual, solution, damping, precond,
    solution_new, residual_new, pre_new, norm_block, old_norm, summed,
):
    params, count = direction.shape
    devices = arrived.shape[0]
    per = LANES // cap
    groups = devices // per
    highs = count // LANES
    low_id = iota((LANES, LANES), 0)

    def body(j, first):
        rows = blocks_to_rows(arrived[at_rows(j, per), :], cap, params)
        row = served[:, at_group(j)]
        at_low = (spread(row % LANES, LANES) == low_id).astype(jnp.float32).astype(jnp.bfloat16)
        high = spread(row // LANES)
        picked = jnp.concatenate([jnp.where(high == h, rows, 0.0) for h in range(highs)], axis=0)
        total = None
        for piece in split_bf16(picked, 3):
            part = lax.dot_general(
                piece, at_low, (((1,), (1,)), ((), ())), preferred_element_type=jnp.float32
            )
            total = part if total is None else total + part
        summed[...] = total if first else summed[...] + total

    body(0, True)
    if groups <= 8:
        for j in range(1, groups):
            body(j, False)
    else:
        lax.fori_loop(1, groups, lambda j, c: (body(j, False), c)[1], 0)

    totals = jnp.sum(arrived[...], axis=0, keepdims=True)
    old = totals[:, params * cap : params * cap + 1]
    curv = totals[:, params * cap + 1 : params * cap + 2]
    step_size = old / curv
    step = jnp.broadcast_to(step_size, (params, LANES))
    new = jnp.zeros((params, LANES), jnp.float32)
    for h in range(highs):
        at = slice(h * LANES, (h + 1) * LANES)
        dire = direction[:, at]
        image = damping[:, at] * dire + summed[h * SUBS : h * SUBS + params, :]
        solution_new[:, at] = solution[:, at] + step * dire
        res = residual[:, at] - step * image
        residual_new[:, at] = res
        pre = apply_precond([precond[k, :, at] for k in range(params)], res)
        pre_new[:, at] = pre
        new = new + res * pre
    norm_block[...] = jnp.broadcast_to(jnp.sum(new), norm_block.shape)
    old_norm[...] = jnp.broadcast_to(old, old_norm.shape)


def final_kernel(norm_blocks, old_norm, direction, pre_new, direction_new):
    new = jnp.sum(norm_blocks[...], axis=0, keepdims=True)
    ratio = new / old_norm[0:1, :]
    params, count = direction.shape
    ratio = jnp.broadcast_to(ratio, (params, LANES))
    for h in range(count // LANES):
        at = slice(h * LANES, (h + 1) * LANES)
        direction_new[:, at] = pre_new[:, at] + ratio * direction[:, at]


def call(kernel, outs, scratch=(), cost=0):
    shapes = [jax.ShapeDtypeStruct(o, jnp.float32) for o in outs]
    return pl.pallas_call(
        kernel,
        out_shape=shapes[0] if len(shapes) == 1 else shapes,
        scratch_shapes=scratch,
        compiler_params=pltpu.CompilerParams(vmem_limit_bytes=32 * 1024 * 1024),
        cost_estimate=pl.CostEstimate(flops=cost, bytes_accessed=cost, transcendentals=0),
    )


def exchange(blocks):
    return lax.all_to_all(blocks, AXES, split_axis=0, concat_axis=0, tiled=True)


def on_device(
    jacobians,
    direction,
    residual,
    solution,
    cam_damping,
    precond,
    land_damping,
    obs_slot,
    obs_mask,
    serve_rows,
):
    devices = lax.axis_size("track") * lax.axis_size("ses")
    params = direction.shape[0]
    cap = serve_rows.shape[1] // devices
    block = (devices, LANES)

    outgoing = call(functools.partial(serve_kernel, cap), [block], cost=400_000)(direction, serve_rows)
    incoming = exchange(outgoing)
    norms = call(norms_kernel, [(SUBS, LANES)], cost=2_000_000)(direction, residual, cam_damping, precond)
    returned = call(
        functools.partial(track_kernel, cap, params),
        [block],
        scratch=[pltpu.VMEM((SUBS, devices * cap), jnp.float32)],
        cost=2_000_000,
    )(incoming, jacobians, obs_slot, obs_mask, land_damping.reshape(1, -1), norms)
    arrived = exchange(returned)
    solution_new, residual_new, pre_new, norm_block, old_norm = call(
        functools.partial(owner_kernel, cap),
        [direction.shape, direction.shape, direction.shape, block, (SUBS, LANES)],
        scratch=[pltpu.VMEM((direction.shape[1] // LANES * SUBS, LANES), jnp.float32)],
        cost=2_000_000,
    )(arrived, serve_rows, direction, residual, solution, cam_damping, precond)
    norm_blocks = exchange(norm_block)
    direction_new = call(final_kernel, [direction.shape], cost=400_000)(
        norm_blocks, old_norm, direction, pre_new
    )
    return (solution_new, residual_new, direction_new)


def solution(mesh):
    return jax.shard_map(
        on_device,
        mesh=mesh,
        in_specs=(
            P(None, None, None, AXES),
            P(None, AXES),
            P(None, AXES),
            P(None, AXES),
            P(None, AXES),
            P(None, None, AXES),
            P(AXES),
            P(None, AXES),
            P(None, AXES),
            P(AXES, None),
        ),
        out_specs=(P(None, AXES), P(None, AXES), P(None, AXES)),
        check_vma=False,
    )
```

```python
import functools

import jax
import jax.numpy as jnp
from jax import lax
from jax.experimental import pallas as pl
from jax.experimental.pallas import tpu as pltpu
from jax.sharding import PartitionSpec as P

LANES = 128
SUBS = 8
AXES = ("track", "ses")


def lane_gather(rows, index):
    return jnp.take_along_axis(rows, index, axis=1, mode="promise_in_bounds")


def spread(row, subs=SUBS):
    return jnp.broadcast_to(row, (subs, row.shape[1]))


def iota(shape, dim):
    return lax.broadcasted_iota(jnp.int32, shape, dim)


def each(count, body):
    if count <= 8:
        for j in range(count):
            body(j)
    else:
        lax.fori_loop(0, count, lambda j, c: (body(j), c)[1], 0)


def at_group(j):
    if isinstance(j, int):
        return pl.ds(j * LANES, LANES)
    return pl.ds(pl.multiple_of(j * LANES, LANES), LANES)


def at_rows(j, size=SUBS):
    if isinstance(j, int):
        return pl.ds(j * size, size)
    return pl.ds(pl.multiple_of(j * size, size), size)


def rows_to_blocks(rows, cap, params):
    per = LANES // cap
    lane = iota((per, LANES), 1)
    index = iota((per, LANES), 0) * cap + lane % cap
    out = jnp.zeros((per, LANES), rows.dtype)
    for k in range(params):
        picked = lane_gather(spread(rows[k : k + 1], per), index)
        out = jnp.where(lane // cap == k, picked, out)
    return out


def blocks_to_rows(blocks, cap, params):
    per = LANES // cap
    lane = iota((SUBS, LANES), 1)
    sub = iota((SUBS, LANES), 0)
    index = jnp.minimum(sub, params - 1) * cap + lane % cap
    out = jnp.zeros((SUBS, LANES), blocks.dtype)
    for src in range(per):
        picked = lane_gather(spread(blocks[src : src + 1]), index)
        out = jnp.where(lane // cap == src, picked, out)
    return jnp.where(sub < params, out, 0.0)


def split_bf16(value, parts):
    pieces = []
    rest = value
    for p in range(parts):
        piece = rest.astype(jnp.bfloat16)
        pieces.append(piece)
        if p + 1 < parts:
            rest = rest - piece.astype(jnp.float32)
    return pieces


def apply_precond(precond, vector):
    params = vector.shape[0]
    total = precond[0] * vector[0:1]
    for k in range(1, params):
        total = total + precond[k] * vector[k : k + 1]
    return total


def serve_kernel(cap, direction_far, served_far, outgoing, direction, served, table, sems):
    params, count = direction.shape
    groups = served.shape[1] // LANES
    per = LANES // cap
    cuts = sems.shape[0] - 1
    width = count // cuts
    head = pltpu.make_async_copy(served_far, served, sems.at[cuts])
    head.start()
    pieces = []
    for c in range(cuts):
        at = pl.ds(c * width, width)
        pieces.append(
            pltpu.make_async_copy(direction_far.at[:, at], direction.at[:, at], sems.at[c])
        )
        pieces[-1].start()
    head.wait()

    for c in range(cuts):
        pieces[c].wait()

        def body(j):
            row = served[:, at_group(j)]
            low = spread(row % LANES, params)
            high = spread(row // LANES, params)
            if c == 0:
                rows = jnp.zeros((params, LANES), jnp.float32)
            else:
                rows = table[:, at_group(j)]
            for h in range(c * width // LANES, (c + 1) * width // LANES):
                picked = lane_gather(direction[:, h * LANES : (h + 1) * LANES], low)
                rows = jnp.where(high == h, picked, rows)
            if c + 1 < cuts:
                table[:, at_group(j)] = rows
            else:
                outgoing[at_rows(j, per), :] = rows_to_blocks(rows, cap, params)

        each(groups, body)


def norms_kernel(
    direction_far, residual_far, damping_far, precond_far, norms,
    direction, residual, damping, precond, sems,
):
    params, count = direction.shape
    pairs = [
        (precond_far, precond),
        (residual_far, residual),
        (direction_far, direction),
        (damping_far, damping),
    ]
    copies = [pltpu.make_async_copy(far, near, sems.at[i]) for i, (far, near) in enumerate(pairs)]
    for copy in copies:
        copy.start()
    for copy in copies:
        copy.wait()
    old = jnp.zeros((params, LANES), jnp.float32)
    curv = jnp.zeros((params, LANES), jnp.float32)
    for h in range(count // LANES):
        at = slice(h * LANES, (h + 1) * LANES)
        res = residual[:, at]
        pre = apply_precond([precond[k, :, at] for k in range(params)], res)
        old = old + res * pre
        dire = direction[:, at]
        curv = curv + damping[:, at] * dire * dire
    row = iota((SUBS, LANES), 0)
    norms[...] = jnp.where(row == 0, jnp.sum(old), jnp.where(row == 1, jnp.sum(curv), 0.0))


def track_kernel(cap, params, incoming, jac, slots, mask, damp, norms, returned, table):
    devices = incoming.shape[0]
    per = LANES // cap
    groups = devices // per
    obs, tracks = slots.shape

    def fill(j):
        table[:, at_group(j)] = blocks_to_rows(incoming[at_rows(j, per), :], cap, params)

    each(groups, fill)

    slot = slots[...]
    owner = slot // cap
    within = slot % cap
    halves = [slice(t * LANES, (t + 1) * LANES) for t in range(tracks // LANES)]
    low = [slot[:, at] % LANES for at in halves]
    high = [slot[:, at] // LANES for at in halves]

    def look(j, camera):
        rows = table[:, at_group(j)]
        out = []
        for k in range(params):
            source = spread(rows[k : k + 1], obs)
            for t in range(len(halves)):
                picked = lane_gather(source, low[t])
                out.append(jnp.where(high[t] == j, picked, camera[len(out)]))
        return tuple(out)

    camera = tuple(jnp.zeros((obs, LANES), jnp.float32) for _ in range(params * len(halves)))
    if groups <= 8:
        for j in range(groups):
            camera = look(j, camera)
    else:
        camera = lax.fori_loop(0, groups, look, camera)
    camera = [
        jnp.concatenate(camera[k * len(halves) : (k + 1) * len(halves)], axis=1)
        for k in range(params)
    ]

    live = mask[...].astype(jnp.float32)
    cam = [[jac[a, k] for k in range(params)] for a in range(2)]
    land = [[jac[a, params + i] for i in range(3)] for a in range(2)]
    projected = []
    for a in range(2):
        total = cam[a][0] * camera[0]
        for k in range(1, params):
            total = total + cam[a][k] * camera[k]
        projected.append(total)
    weighted = [[land[a][i] * live for i in range(3)] for a in range(2)]

    def over_slots(value):
        return jnp.sum(value, axis=0, keepdims=True)

    normal = {}
    for i in range(3):
        for j in range(i, 3):
            entry = over_slots(weighted[0][i] * land[0][j] + weighted[1][i] * land[1][j])
            if i == j:
                entry = entry + damp[...]
            normal[i, j] = entry
            normal[j, i] = entry
    rhs = [over_slots(weighted[0][i] * projected[0] + weighted[1][i] * projected[1]) for i in range(3)]
    cof = [
        [
            normal[(i + 1) % 3, (j + 1) % 3] * normal[(i + 2) % 3, (j + 2) % 3]
            - normal[(i + 1) % 3, (j + 2) % 3] * normal[(i + 2) % 3, (j + 1) % 3]
            for j in range(3)
        ]
        for i in range(3)
    ]
    det = normal[0, 0] * cof[0][0] + normal[0, 1] * cof[0][1] + normal[0, 2] * cof[0][2]
    step = [
        (cof[0][i] * rhs[0] + cof[1][i] * rhs[1] + cof[2][i] * rhs[2]) / det for i in range(3)
    ]
    res = [
        live
        * (projected[a] - (land[a][0] * step[0] + land[a][1] * step[1] + land[a][2] * step[2]))
        for a in range(2)
    ]
    curv = jnp.sum(res[0] * projected[0] + res[1] * projected[1])
    grad = [cam[0][k] * res[0] + cam[1][k] * res[1] for k in range(params)]

    owner_id = iota((devices, tracks), 0)
    within_id = iota((cap, tracks), 0)
    total = jnp.zeros((devices, LANES), jnp.float32)
    pad = LANES - params * cap
    for o in range(obs):
        at_owner = (spread(owner[o : o + 1], devices) == owner_id).astype(jnp.float32).astype(jnp.bfloat16)
        at_within = spread(within[o : o + 1], cap) == within_id
        values = [jnp.where(at_within, spread(grad[k][o : o + 1], cap), 0.0) for k in range(params)]
        if pad:
            values.append(jnp.zeros((pad, tracks), jnp.float32))
        values = jnp.concatenate(values, axis=0)
        for piece in split_bf16(values, 3):
            total = total + lax.dot_general(
                at_owner, piece, (((1,), (1,)), ((), ())), preferred_element_type=jnp.float32
            )
    lane = iota((devices, LANES), 1)
    old_part = spread(norms[0:1, :], devices)
    curv_part = spread(norms[1:2, :], devices) + curv
    total = jnp.where(lane == params * cap, old_part, total)
    returned[...] = jnp.where(lane == params * cap + 1, curv_part, total)


def owner_kernel(
    cap, arrived, served, direction, residual, solution, damping, precond,
    solution_new, residual_new, pre_new, norm_block, old_norm, summed,
):
    params, count = direction.shape
    devices = arrived.shape[0]
    per = LANES // cap
    groups = devices // per
    highs = count // LANES
    low_id = iota((LANES, LANES), 0)

    def body(j, first):
        rows = blocks_to_rows(arrived[at_rows(j, per), :], cap, params)
        row = served[:, at_group(j)]
        at_low = (spread(row % LANES, LANES) == low_id).astype(jnp.float32).astype(jnp.bfloat16)
        high = spread(row // LANES)
        picked = jnp.concatenate([jnp.where(high == h, rows, 0.0) for h in range(highs)], axis=0)
        total = None
        for piece in split_bf16(picked, 3):
            part = lax.dot_general(
                piece, at_low, (((1,), (1,)), ((), ())), preferred_element_type=jnp.float32
            )
            total = part if total is None else total + part
        summed[...] = total if first else summed[...] + total

    body(0, True)
    if groups <= 8:
        for j in range(1, groups):
            body(j, False)
    else:
        lax.fori_loop(1, groups, lambda j, c: (body(j, False), c)[1], 0)

    totals = jnp.sum(arrived[...], axis=0, keepdims=True)
    old = totals[:, params * cap : params * cap + 1]
    curv = totals[:, params * cap + 1 : params * cap + 2]
    step_size = old / curv
    step = jnp.broadcast_to(step_size, (params, LANES))
    new = jnp.zeros((params, LANES), jnp.float32)
    for h in range(highs):
        at = slice(h * LANES, (h + 1) * LANES)
        dire = direction[:, at]
        image = damping[:, at] * dire + summed[h * SUBS : h * SUBS + params, :]
        solution_new[:, at] = solution[:, at] + step * dire
        res = residual[:, at] - step * image
        residual_new[:, at] = res
        pre = apply_precond([precond[k, :, at] for k in range(params)], res)
        pre_new[:, at] = pre
        new = new + res * pre
    norm_block[...] = jnp.broadcast_to(jnp.sum(new), norm_block.shape)
    old_norm[...] = jnp.broadcast_to(old, old_norm.shape)


def final_kernel(norm_blocks, old_norm, direction, pre_new, direction_new):
    new = jnp.sum(norm_blocks[...], axis=0, keepdims=True)
    ratio = new / old_norm[0:1, :]
    params, count = direction.shape
    ratio = jnp.broadcast_to(ratio, (params, LANES))
    for h in range(count // LANES):
        at = slice(h * LANES, (h + 1) * LANES)
        direction_new[:, at] = pre_new[:, at] + ratio * direction[:, at]


def call(kernel, outs, scratch=(), cost=0, far=0):
    shapes = [jax.ShapeDtypeStruct(o, jnp.float32) for o in outs]
    places = {"in_specs": [pl.BlockSpec(memory_space=pltpu.HBM)] * far} if far else {}
    run = pl.pallas_call(
        kernel,
        **places,
        out_shape=shapes[0] if len(shapes) == 1 else shapes,
        scratch_shapes=scratch,
        compiler_params=pltpu.CompilerParams(vmem_limit_bytes=32 * 1024 * 1024),
        cost_estimate=pl.CostEstimate(flops=cost, bytes_accessed=cost, transcendentals=0),
    )
    if not far:
        return run
    return lambda *args: run(*[pltpu.with_memory_space_constraint(a, pltpu.HBM) for a in args])


def exchange(blocks):
    return lax.all_to_all(blocks, AXES, split_axis=0, concat_axis=0, tiled=True)


def on_device(
    jacobians,
    direction,
    residual,
    solution,
    cam_damping,
    precond,
    land_damping,
    obs_slot,
    obs_mask,
    serve_rows,
):
    devices = lax.axis_size("track") * lax.axis_size("ses")
    params = direction.shape[0]
    cap = serve_rows.shape[1] // devices
    block = (devices, LANES)

    local = pltpu.VMEM(direction.shape, jnp.float32)
    outgoing = call(
        functools.partial(serve_kernel, cap),
        [block],
        scratch=[
            local,
            pltpu.VMEM(serve_rows.shape, jnp.int32),
            pltpu.VMEM((params, serve_rows.shape[1]), jnp.float32),
            pltpu.SemaphoreType.DMA((5,)),
        ],
        cost=400_000,
        far=2,
    )(direction, serve_rows)
    incoming = exchange(outgoing)
    norms = call(
        norms_kernel,
        [(SUBS, LANES)],
        scratch=[
            local,
            local,
            local,
            pltpu.VMEM(precond.shape, jnp.float32),
            pltpu.SemaphoreType.DMA((4,)),
        ],
        cost=2_000_000,
        far=4,
    )(direction, residual, cam_damping, precond)
    returned = call(
        functools.partial(track_kernel, cap, params),
        [block],
        scratch=[pltpu.VMEM((SUBS, devices * cap), jnp.float32)],
        cost=2_000_000,
    )(incoming, jacobians, obs_slot, obs_mask, land_damping.reshape(1, -1), norms)
    arrived = exchange(returned)
    solution_new, residual_new, pre_new, norm_block, old_norm = call(
        functools.partial(owner_kernel, cap),
        [direction.shape, direction.shape, direction.shape, block, (SUBS, LANES)],
        scratch=[pltpu.VMEM((direction.shape[1] // LANES * SUBS, LANES), jnp.float32)],
        cost=2_000_000,
    )(arrived, serve_rows, direction, residual, solution, cam_damping, precond)
    norm_blocks = exchange(norm_block)
    direction_new = call(final_kernel, [direction.shape], cost=400_000)(
        norm_blocks, old_norm, direction, pre_new
    )
    return (solution_new, residual_new, direction_new)


def solution(mesh):
    return jax.shard_map(
        on_device,
        mesh=mesh,
        in_specs=(
            P(None, None, None, AXES),
            P(None, AXES),
            P(None, AXES),
            P(None, AXES),
            P(None, AXES),
            P(None, None, AXES),
            P(AXES),
            P(None, AXES),
            P(None, AXES),
            P(AXES, None),
        ),
        out_specs=(P(None, AXES), P(None, AXES), P(None, AXES)),
        check_vma=False,
    )
```

```python
import functools

import jax
import jax.numpy as jnp
from jax import lax
from jax.experimental import pallas as pl
from jax.experimental.pallas import tpu as pltpu
from jax.sharding import PartitionSpec as P

LANES = 128
SUBS = 8
AXES = ("track", "ses")


def lane_gather(rows, index):
    return jnp.take_along_axis(rows, index, axis=1, mode="promise_in_bounds")


def spread(row, subs=SUBS):
    return jnp.broadcast_to(row, (subs, row.shape[1]))


def iota(shape, dim):
    return lax.broadcasted_iota(jnp.int32, shape, dim)


def each(count, body):
    if count <= 8:
        for j in range(count):
            body(j)
    else:
        lax.fori_loop(0, count, lambda j, c: (body(j), c)[1], 0)


def at_group(j):
    if isinstance(j, int):
        return pl.ds(j * LANES, LANES)
    return pl.ds(pl.multiple_of(j * LANES, LANES), LANES)


def at_rows(j, size=SUBS):
    if isinstance(j, int):
        return pl.ds(j * size, size)
    return pl.ds(pl.multiple_of(j * size, size), size)


def rows_to_blocks(rows, cap, params):
    per = LANES // cap
    lane = iota((per, LANES), 1)
    index = iota((per, LANES), 0) * cap + lane % cap
    out = jnp.zeros((per, LANES), rows.dtype)
    for k in range(params):
        picked = lane_gather(spread(rows[k : k + 1], per), index)
        out = jnp.where(lane // cap == k, picked, out)
    return out


def blocks_to_rows(blocks, cap, params):
    per = LANES // cap
    lane = iota((SUBS, LANES), 1)
    sub = iota((SUBS, LANES), 0)
    index = jnp.minimum(sub, params - 1) * cap + lane % cap
    out = jnp.zeros((SUBS, LANES), blocks.dtype)
    for src in range(per):
        picked = lane_gather(spread(blocks[src : src + 1]), index)
        out = jnp.where(lane // cap == src, picked, out)
    return jnp.where(sub < params, out, 0.0)


def split_bf16(value, parts):
    pieces = []
    rest = value
    for p in range(parts):
        piece = rest.astype(jnp.bfloat16)
        pieces.append(piece)
        if p + 1 < parts:
            rest = rest - piece.astype(jnp.float32)
    return pieces


def apply_precond(precond, vector):
    params = vector.shape[0]
    total = precond[0] * vector[0:1]
    for k in range(1, params):
        total = total + precond[k] * vector[k : k + 1]
    return total


def serve_kernel(cap, direction_far, served_far, outgoing, direction, served, table, sems):
    params, count = direction.shape
    groups = served.shape[1] // LANES
    per = LANES // cap
    cuts = sems.shape[0] - 1
    width = count // cuts
    head = pltpu.make_async_copy(served_far, served, sems.at[cuts])
    head.start()
    pieces = []
    for c in range(cuts):
        at = pl.ds(c * width, width)
        pieces.append(
            pltpu.make_async_copy(direction_far.at[:, at], direction.at[:, at], sems.at[c])
        )
        pieces[-1].start()
    head.wait()

    for c in range(cuts):
        pieces[c].wait()

        def body(j):
            row = served[:, at_group(j)]
            low = spread(row % LANES, params)
            high = spread(row // LANES, params)
            if c == 0:
                rows = jnp.zeros((params, LANES), jnp.float32)
            else:
                rows = table[:, at_group(j)]
            for h in range(c * width // LANES, (c + 1) * width // LANES):
                picked = lane_gather(direction[:, h * LANES : (h + 1) * LANES], low)
                rows = jnp.where(high == h, picked, rows)
            if c + 1 < cuts:
                table[:, at_group(j)] = rows
            else:
                outgoing[at_rows(j, per), :] = rows_to_blocks(rows, cap, params)

        each(groups, body)


def norms_kernel(
    direction_far, residual_far, damping_far, precond_far, norms,
    direction, residual, damping, precond, sems,
):
    params, count = direction.shape
    pairs = [
        (precond_far, precond),
        (residual_far, residual),
        (direction_far, direction),
        (damping_far, damping),
    ]
    copies = [pltpu.make_async_copy(far, near, sems.at[i]) for i, (far, near) in enumerate(pairs)]
    for copy in copies:
        copy.start()
    for copy in copies:
        copy.wait()
    old = jnp.zeros((params, LANES), jnp.float32)
    curv = jnp.zeros((params, LANES), jnp.float32)
    for h in range(count // LANES):
        at = slice(h * LANES, (h + 1) * LANES)
        res = residual[:, at]
        pre = apply_precond([precond[k, :, at] for k in range(params)], res)
        old = old + res * pre
        dire = direction[:, at]
        curv = curv + damping[:, at] * dire * dire
    row = iota((SUBS, LANES), 0)
    norms[...] = jnp.where(row == 0, jnp.sum(old), jnp.where(row == 1, jnp.sum(curv), 0.0))


def track_kernel(cap, params, incoming, jac, slots, mask, damp, norms, returned, table):
    devices = incoming.shape[0]
    per = LANES // cap
    groups = devices // per
    obs, tracks = slots.shape

    def fill(j):
        table[:, at_group(j)] = blocks_to_rows(incoming[at_rows(j, per), :], cap, params)

    each(groups, fill)

    slot = slots[...]
    owner = slot // cap
    within = slot % cap
    halves = [slice(t * LANES, (t + 1) * LANES) for t in range(tracks // LANES)]
    low = [slot[:, at] % LANES for at in halves]
    high = [slot[:, at] // LANES for at in halves]

    def look(j, camera):
        rows = table[:, at_group(j)]
        out = []
        for k in range(params):
            source = spread(rows[k : k + 1], obs)
            for t in range(len(halves)):
                picked = lane_gather(source, low[t])
                out.append(jnp.where(high[t] == j, picked, camera[len(out)]))
        return tuple(out)

    camera = tuple(jnp.zeros((obs, LANES), jnp.float32) for _ in range(params * len(halves)))
    if groups <= 8:
        for j in range(groups):
            camera = look(j, camera)
    else:
        camera = lax.fori_loop(0, groups, look, camera)
    camera = [
        jnp.concatenate(camera[k * len(halves) : (k + 1) * len(halves)], axis=1)
        for k in range(params)
    ]

    live = mask[...].astype(jnp.float32)
    cam = [[jac[a, k] for k in range(params)] for a in range(2)]
    land = [[jac[a, params + i] for i in range(3)] for a in range(2)]
    projected = []
    for a in range(2):
        total = cam[a][0] * camera[0]
        for k in range(1, params):
            total = total + cam[a][k] * camera[k]
        projected.append(total)
    weighted = [[land[a][i] * live for i in range(3)] for a in range(2)]

    def over_slots(value):
        return jnp.sum(value, axis=0, keepdims=True)

    normal = {}
    for i in range(3):
        for j in range(i, 3):
            entry = over_slots(weighted[0][i] * land[0][j] + weighted[1][i] * land[1][j])
            if i == j:
                entry = entry + damp[...]
            normal[i, j] = entry
            normal[j, i] = entry
    rhs = [over_slots(weighted[0][i] * projected[0] + weighted[1][i] * projected[1]) for i in range(3)]
    cof = [
        [
            normal[(i + 1) % 3, (j + 1) % 3] * normal[(i + 2) % 3, (j + 2) % 3]
            - normal[(i + 1) % 3, (j + 2) % 3] * normal[(i + 2) % 3, (j + 1) % 3]
            for j in range(3)
        ]
        for i in range(3)
    ]
    det = normal[0, 0] * cof[0][0] + normal[0, 1] * cof[0][1] + normal[0, 2] * cof[0][2]
    step = [
        (cof[0][i] * rhs[0] + cof[1][i] * rhs[1] + cof[2][i] * rhs[2]) / det for i in range(3)
    ]
    res = [
        live
        * (projected[a] - (land[a][0] * step[0] + land[a][1] * step[1] + land[a][2] * step[2]))
        for a in range(2)
    ]
    curv = jnp.sum(res[0] * projected[0] + res[1] * projected[1])
    grad = [cam[0][k] * res[0] + cam[1][k] * res[1] for k in range(params)]

    owner_id = iota((devices, tracks), 0)
    within_id = iota((cap, tracks), 0)
    total = jnp.zeros((devices, LANES), jnp.float32)
    pad = LANES - params * cap
    for o in range(obs):
        at_owner = (spread(owner[o : o + 1], devices) == owner_id).astype(jnp.float32).astype(jnp.bfloat16)
        at_within = spread(within[o : o + 1], cap) == within_id
        values = [jnp.where(at_within, spread(grad[k][o : o + 1], cap), 0.0) for k in range(params)]
        if pad:
            values.append(jnp.zeros((pad, tracks), jnp.float32))
        values = jnp.concatenate(values, axis=0)
        for piece in split_bf16(values, 3):
            total = total + lax.dot_general(
                at_owner, piece, (((1,), (1,)), ((), ())), preferred_element_type=jnp.float32
            )
    lane = iota((devices, LANES), 1)
    old_part = spread(norms[0:1, :], devices)
    curv_part = spread(norms[1:2, :], devices) + curv
    total = jnp.where(lane == params * cap, old_part, total)
    returned[...] = jnp.where(lane == params * cap + 1, curv_part, total)


def owner_kernel(
    cap, arrived, served, direction, residual, solution, damping, precond,
    solution_new, residual_new, pre_new, norm_block, old_norm, summed,
):
    params, count = direction.shape
    devices = arrived.shape[0]
    per = LANES // cap
    groups = devices // per
    highs = count // LANES
    low_id = iota((LANES, LANES), 0)

    def body(j, first):
        rows = blocks_to_rows(arrived[at_rows(j, per), :], cap, params)
        row = served[:, at_group(j)]
        at_low = (spread(row % LANES, LANES) == low_id).astype(jnp.float32).astype(jnp.bfloat16)
        high = spread(row // LANES)
        picked = jnp.concatenate([jnp.where(high == h, rows, 0.0) for h in range(highs)], axis=0)
        total = None
        for piece in split_bf16(picked, 3):
            part = lax.dot_general(
                piece, at_low, (((1,), (1,)), ((), ())), preferred_element_type=jnp.float32
            )
            total = part if total is None else total + part
        summed[...] = total if first else summed[...] + total

    body(0, True)
    if groups <= 8:
        for j in range(1, groups):
            body(j, False)
    else:
        lax.fori_loop(1, groups, lambda j, c: (body(j, False), c)[1], 0)

    totals = jnp.sum(arrived[...], axis=0, keepdims=True)
    old = totals[:, params * cap : params * cap + 1]
    curv = totals[:, params * cap + 1 : params * cap + 2]
    step_size = old / curv
    step = jnp.broadcast_to(step_size, (params, LANES))
    new = jnp.zeros((params, LANES), jnp.float32)
    for h in range(highs):
        at = slice(h * LANES, (h + 1) * LANES)
        dire = direction[:, at]
        image = damping[:, at] * dire + summed[h * SUBS : h * SUBS + params, :]
        solution_new[:, at] = solution[:, at] + step * dire
        res = residual[:, at] - step * image
        residual_new[:, at] = res
        pre = apply_precond([precond[k, :, at] for k in range(params)], res)
        pre_new[:, at] = pre
        new = new + res * pre
    norm_block[...] = jnp.broadcast_to(jnp.sum(new), norm_block.shape)
    old_norm[...] = jnp.broadcast_to(old, old_norm.shape)


def final_kernel(new_norm, old_norm, direction, pre_new, direction_new):
    ratio = new_norm[0:1, :] / old_norm[0:1, :]
    params, count = direction.shape
    ratio = jnp.broadcast_to(ratio, (params, LANES))
    for h in range(count // LANES):
        at = slice(h * LANES, (h + 1) * LANES)
        direction_new[:, at] = pre_new[:, at] + ratio * direction[:, at]


def call(kernel, outs, scratch=(), cost=0, far=0):
    shapes = [jax.ShapeDtypeStruct(o, jnp.float32) for o in outs]
    places = {"in_specs": [pl.BlockSpec(memory_space=pltpu.HBM)] * far} if far else {}
    run = pl.pallas_call(
        kernel,
        **places,
        out_shape=shapes[0] if len(shapes) == 1 else shapes,
        scratch_shapes=scratch,
        compiler_params=pltpu.CompilerParams(vmem_limit_bytes=32 * 1024 * 1024),
        cost_estimate=pl.CostEstimate(flops=cost, bytes_accessed=cost, transcendentals=0),
    )
    if not far:
        return run
    return lambda *args: run(*[pltpu.with_memory_space_constraint(a, pltpu.HBM) for a in args])


def exchange(blocks):
    return lax.all_to_all(blocks, AXES, split_axis=0, concat_axis=0, tiled=True)


def digits(count):
    out = []
    while count > 1:
        radix = 8 if count % 8 == 0 and count != 32 else 4 if count % 4 == 0 else 2
        out.append(radix)
        count //= radix
    return out


def sum_everywhere(value, devices):
    stride = 1
    for radix in digits(devices):
        def moved(d, shift):
            digit = d // stride % radix
            return d + ((digit + shift) % radix - digit) * stride

        total = value
        for shift in range(1, radix):
            perm = [(d, moved(d, shift)) for d in range(devices)]
            total = total + lax.ppermute(value, AXES, perm)
        value = total
        stride *= radix
    return value


def on_device(
    jacobians,
    direction,
    residual,
    solution,
    cam_damping,
    precond,
    land_damping,
    obs_slot,
    obs_mask,
    serve_rows,
):
    devices = lax.axis_size("track") * lax.axis_size("ses")
    params = direction.shape[0]
    cap = serve_rows.shape[1] // devices
    block = (devices, LANES)

    local = pltpu.VMEM(direction.shape, jnp.float32)
    outgoing = call(
        functools.partial(serve_kernel, cap),
        [block],
        scratch=[
            local,
            pltpu.VMEM(serve_rows.shape, jnp.int32),
            pltpu.VMEM((params, serve_rows.shape[1]), jnp.float32),
            pltpu.SemaphoreType.DMA((5,)),
        ],
        cost=400_000,
        far=2,
    )(direction, serve_rows)
    incoming = exchange(outgoing)
    norms = call(
        norms_kernel,
        [(SUBS, LANES)],
        scratch=[
            local,
            local,
            local,
            pltpu.VMEM(precond.shape, jnp.float32),
            pltpu.SemaphoreType.DMA((4,)),
        ],
        cost=2_000_000,
        far=4,
    )(direction, residual, cam_damping, precond)
    returned = call(
        functools.partial(track_kernel, cap, params),
        [block],
        scratch=[pltpu.VMEM((SUBS, devices * cap), jnp.float32)],
        cost=2_000_000,
    )(incoming, jacobians, obs_slot, obs_mask, land_damping.reshape(1, -1), norms)
    arrived = exchange(returned)
    solution_new, residual_new, pre_new, norm_block, old_norm = call(
        functools.partial(owner_kernel, cap),
        [direction.shape, direction.shape, direction.shape, (SUBS, LANES), (SUBS, LANES)],
        scratch=[pltpu.VMEM((direction.shape[1] // LANES * SUBS, LANES), jnp.float32)],
        cost=2_000_000,
    )(arrived, serve_rows, direction, residual, solution, cam_damping, precond)
    new_norm = sum_everywhere(norm_block, devices)
    direction_new = call(final_kernel, [direction.shape], cost=400_000)(
        new_norm, old_norm, direction, pre_new
    )
    return (solution_new, residual_new, direction_new)


def solution(mesh):
    return jax.shard_map(
        on_device,
        mesh=mesh,
        in_specs=(
            P(None, None, None, AXES),
            P(None, AXES),
            P(None, AXES),
            P(None, AXES),
            P(None, AXES),
            P(None, None, AXES),
            P(AXES),
            P(None, AXES),
            P(None, AXES),
            P(AXES, None),
        ),
        out_specs=(P(None, AXES), P(None, AXES), P(None, AXES)),
        check_vma=False,
    )
```

```python
import functools

import jax
import jax.numpy as jnp
from jax import lax
from jax.experimental import pallas as pl
from jax.experimental.pallas import tpu as pltpu
from jax.sharding import PartitionSpec as P

LANES = 128
SUBS = 8
AXES = ("track", "ses")


def lane_gather(rows, index):
    return jnp.take_along_axis(rows, index, axis=1, mode="promise_in_bounds")


def spread(row, subs=SUBS):
    return jnp.broadcast_to(row, (subs, row.shape[1]))


def iota(shape, dim):
    return lax.broadcasted_iota(jnp.int32, shape, dim)


def each(count, body):
    if count <= 8:
        for j in range(count):
            body(j)
    else:
        lax.fori_loop(0, count, lambda j, c: (body(j), c)[1], 0)


def at_group(j):
    if isinstance(j, int):
        return pl.ds(j * LANES, LANES)
    return pl.ds(pl.multiple_of(j * LANES, LANES), LANES)


def at_rows(j, size=SUBS):
    if isinstance(j, int):
        return pl.ds(j * size, size)
    return pl.ds(pl.multiple_of(j * size, size), size)


def rows_to_blocks(rows, cap, params):
    per = LANES // cap
    lane = iota((per, LANES), 1)
    index = iota((per, LANES), 0) * cap + lane % cap
    out = jnp.zeros((per, LANES), rows.dtype)
    for k in range(params):
        picked = lane_gather(spread(rows[k : k + 1], per), index)
        out = jnp.where(lane // cap == k, picked, out)
    return out


def blocks_to_rows(blocks, cap, params):
    per = LANES // cap
    lane = iota((SUBS, LANES), 1)
    sub = iota((SUBS, LANES), 0)
    index = jnp.minimum(sub, params - 1) * cap + lane % cap
    out = jnp.zeros((SUBS, LANES), blocks.dtype)
    for src in range(per):
        picked = lane_gather(spread(blocks[src : src + 1]), index)
        out = jnp.where(lane // cap == src, picked, out)
    return jnp.where(sub < params, out, 0.0)


def split_bf16(value, parts):
    pieces = []
    rest = value
    for p in range(parts):
        piece = rest.astype(jnp.bfloat16)
        pieces.append(piece)
        if p + 1 < parts:
            rest = rest - piece.astype(jnp.float32)
    return pieces


def apply_precond(precond, vector):
    params = vector.shape[0]
    total = precond[0] * vector[0:1]
    for k in range(1, params):
        total = total + precond[k] * vector[k : k + 1]
    return total


def serve_kernel(cap, direction_far, served_far, outgoing, direction, served, table, sems):
    params, count = direction.shape
    groups = served.shape[1] // LANES
    per = LANES // cap
    cuts = sems.shape[0] - 1
    width = count // cuts
    head = pltpu.make_async_copy(served_far, served, sems.at[cuts])
    head.start()
    pieces = []
    for c in range(cuts):
        at = pl.ds(c * width, width)
        pieces.append(
            pltpu.make_async_copy(direction_far.at[:, at], direction.at[:, at], sems.at[c])
        )
        pieces[-1].start()
    head.wait()

    for c in range(cuts):
        pieces[c].wait()

        def body(j):
            row = served[:, at_group(j)]
            low = spread(row % LANES, params)
            high = spread(row // LANES, params)
            if c == 0:
                rows = jnp.zeros((params, LANES), jnp.float32)
            else:
                rows = table[:, at_group(j)]
            for h in range(c * width // LANES, (c + 1) * width // LANES):
                picked = lane_gather(direction[:, h * LANES : (h + 1) * LANES], low)
                rows = jnp.where(high == h, picked, rows)
            if c + 1 < cuts:
                table[:, at_group(j)] = rows
            else:
                outgoing[at_rows(j, per), :] = rows_to_blocks(rows, cap, params)

        each(groups, body)


def norms_kernel(
    direction_far, residual_far, damping_far, precond_far, norms,
    direction, residual, damping, precond, sems,
):
    params, count = direction.shape
    pairs = [
        (precond_far, precond),
        (residual_far, residual),
        (direction_far, direction),
        (damping_far, damping),
    ]
    copies = [pltpu.make_async_copy(far, near, sems.at[i]) for i, (far, near) in enumerate(pairs)]
    for copy in copies:
        copy.start()
    for copy in copies:
        copy.wait()
    old = jnp.zeros((params, LANES), jnp.float32)
    curv = jnp.zeros((params, LANES), jnp.float32)
    for h in range(count // LANES):
        at = slice(h * LANES, (h + 1) * LANES)
        res = residual[:, at]
        pre = apply_precond([precond[k, :, at] for k in range(params)], res)
        old = old + res * pre
        dire = direction[:, at]
        curv = curv + damping[:, at] * dire * dire
    row = iota((SUBS, LANES), 0)
    norms[...] = jnp.where(row == 0, jnp.sum(old), jnp.where(row == 1, jnp.sum(curv), 0.0))


def track_kernel(cap, params, incoming, jac, slots, mask, damp, norms, returned, table):
    devices = incoming.shape[0]
    per = LANES // cap
    groups = devices // per
    obs, tracks = slots.shape

    def fill(j):
        table[:, at_group(j)] = blocks_to_rows(incoming[at_rows(j, per), :], cap, params)

    each(groups, fill)

    slot = slots[...]
    owner = slot // cap
    within = slot % cap
    halves = [slice(t * LANES, (t + 1) * LANES) for t in range(tracks // LANES)]
    low = [slot[:, at] % LANES for at in halves]
    high = [slot[:, at] // LANES for at in halves]

    def look(j, camera):
        rows = table[:, at_group(j)]
        out = []
        for k in range(params):
            source = spread(rows[k : k + 1], obs)
            for t in range(len(halves)):
                picked = lane_gather(source, low[t])
                out.append(jnp.where(high[t] == j, picked, camera[len(out)]))
        return tuple(out)

    camera = tuple(jnp.zeros((obs, LANES), jnp.float32) for _ in range(params * len(halves)))
    if groups <= 8:
        for j in range(groups):
            camera = look(j, camera)
    else:
        camera = lax.fori_loop(0, groups, look, camera)
    camera = [
        jnp.concatenate(camera[k * len(halves) : (k + 1) * len(halves)], axis=1)
        for k in range(params)
    ]

    live = mask[...].astype(jnp.float32)
    cam = [[jac[a, k] for k in range(params)] for a in range(2)]
    land = [[jac[a, params + i] for i in range(3)] for a in range(2)]
    projected = []
    for a in range(2):
        total = cam[a][0] * camera[0]
        for k in range(1, params):
            total = total + cam[a][k] * camera[k]
        projected.append(total)
    weighted = [[land[a][i] * live for i in range(3)] for a in range(2)]

    def over_slots(value):
        return jnp.sum(value, axis=0, keepdims=True)

    normal = {}
    for i in range(3):
        for j in range(i, 3):
            entry = over_slots(weighted[0][i] * land[0][j] + weighted[1][i] * land[1][j])
            if i == j:
                entry = entry + damp[...]
            normal[i, j] = entry
            normal[j, i] = entry
    rhs = [over_slots(weighted[0][i] * projected[0] + weighted[1][i] * projected[1]) for i in range(3)]
    cof = [
        [
            normal[(i + 1) % 3, (j + 1) % 3] * normal[(i + 2) % 3, (j + 2) % 3]
            - normal[(i + 1) % 3, (j + 2) % 3] * normal[(i + 2) % 3, (j + 1) % 3]
            for j in range(3)
        ]
        for i in range(3)
    ]
    det = normal[0, 0] * cof[0][0] + normal[0, 1] * cof[0][1] + normal[0, 2] * cof[0][2]
    step = [
        (cof[0][i] * rhs[0] + cof[1][i] * rhs[1] + cof[2][i] * rhs[2]) / det for i in range(3)
    ]
    res = [
        live
        * (projected[a] - (land[a][0] * step[0] + land[a][1] * step[1] + land[a][2] * step[2]))
        for a in range(2)
    ]
    curv = jnp.sum(res[0] * projected[0] + res[1] * projected[1])
    grad = [cam[0][k] * res[0] + cam[1][k] * res[1] for k in range(params)]

    owner_id = iota((devices, tracks), 0)
    within_id = iota((cap, tracks), 0)
    total = jnp.zeros((devices, LANES), jnp.float32)
    pad = LANES - params * cap
    for o in range(obs):
        at_owner = (spread(owner[o : o + 1], devices) == owner_id).astype(jnp.float32).astype(jnp.bfloat16)
        at_within = spread(within[o : o + 1], cap) == within_id
        values = [jnp.where(at_within, spread(grad[k][o : o + 1], cap), 0.0) for k in range(params)]
        if pad:
            values.append(jnp.zeros((pad, tracks), jnp.float32))
        values = jnp.concatenate(values, axis=0)
        for piece in split_bf16(values, 3):
            total = total + lax.dot_general(
                at_owner, piece, (((1,), (1,)), ((), ())), preferred_element_type=jnp.float32
            )
    lane = iota((devices, LANES), 1)
    old_part = spread(norms[0:1, :], devices)
    curv_part = spread(norms[1:2, :], devices) + curv
    total = jnp.where(lane == params * cap, old_part, total)
    returned[...] = jnp.where(lane == params * cap + 1, curv_part, total)


def owner_kernel(
    cap, arrived, served, direction, residual, solution, damping, precond,
    solution_new, residual_new, pre_new, norm_block, old_norm, summed,
):
    params, count = direction.shape
    devices = arrived.shape[0]
    per = LANES // cap
    groups = devices // per
    highs = count // LANES
    low_id = iota((LANES, LANES), 0)

    def body(j, first):
        rows = blocks_to_rows(arrived[at_rows(j, per), :], cap, params)
        row = served[:, at_group(j)]
        at_low = (spread(row % LANES, LANES) == low_id).astype(jnp.float32).astype(jnp.bfloat16)
        high = spread(row // LANES)
        picked = jnp.concatenate([jnp.where(high == h, rows, 0.0) for h in range(highs)], axis=0)
        total = None
        for piece in split_bf16(picked, 3):
            part = lax.dot_general(
                piece, at_low, (((1,), (1,)), ((), ())), preferred_element_type=jnp.float32
            )
            total = part if total is None else total + part
        summed[...] = total if first else summed[...] + total

    body(0, True)
    if groups <= 8:
        for j in range(1, groups):
            body(j, False)
    else:
        lax.fori_loop(1, groups, lambda j, c: (body(j, False), c)[1], 0)

    totals = jnp.sum(arrived[...], axis=0, keepdims=True)
    old = totals[:, params * cap : params * cap + 1]
    curv = totals[:, params * cap + 1 : params * cap + 2]
    step_size = old / curv
    step = jnp.broadcast_to(step_size, (params, LANES))
    new = jnp.zeros((params, LANES), jnp.float32)
    for h in range(highs):
        at = slice(h * LANES, (h + 1) * LANES)
        dire = direction[:, at]
        image = damping[:, at] * dire + summed[h * SUBS : h * SUBS + params, :]
        solution_new[:, at] = solution[:, at] + step * dire
        res = residual[:, at] - step * image
        residual_new[:, at] = res
        pre = apply_precond([precond[k, :, at] for k in range(params)], res)
        pre_new[:, at] = pre
        new = new + res * pre
    norm_block[...] = jnp.broadcast_to(jnp.sum(new), norm_block.shape)
    old_norm[...] = jnp.broadcast_to(old, old_norm.shape)


def final_kernel(norm_blocks, old_norm, direction, pre_new, direction_new):
    new = jnp.sum(norm_blocks[...], axis=0, keepdims=True)
    ratio = new / old_norm[0:1, :]
    params, count = direction.shape
    ratio = jnp.broadcast_to(ratio, (params, LANES))
    for h in range(count // LANES):
        at = slice(h * LANES, (h + 1) * LANES)
        direction_new[:, at] = pre_new[:, at] + ratio * direction[:, at]


def call(kernel, outs, scratch=(), cost=0, far=0):
    shapes = [jax.ShapeDtypeStruct(o, jnp.float32) for o in outs]
    places = {"in_specs": [pl.BlockSpec(memory_space=pltpu.HBM)] * far} if far else {}
    run = pl.pallas_call(
        kernel,
        **places,
        out_shape=shapes[0] if len(shapes) == 1 else shapes,
        scratch_shapes=scratch,
        compiler_params=pltpu.CompilerParams(vmem_limit_bytes=32 * 1024 * 1024),
        cost_estimate=pl.CostEstimate(flops=cost, bytes_accessed=cost, transcendentals=0),
    )
    if not far:
        return run
    return lambda *args: run(*[pltpu.with_memory_space_constraint(a, pltpu.HBM) for a in args])


def exchange(blocks):
    return lax.all_to_all(blocks, AXES, split_axis=0, concat_axis=0, tiled=True)


def on_device(
    jacobians,
    direction,
    residual,
    solution,
    cam_damping,
    precond,
    land_damping,
    obs_slot,
    obs_mask,
    serve_rows,
):
    devices = lax.axis_size("track") * lax.axis_size("ses")
    params = direction.shape[0]
    cap = serve_rows.shape[1] // devices
    block = (devices, LANES)

    local = pltpu.VMEM(direction.shape, jnp.float32)
    outgoing = call(
        functools.partial(serve_kernel, cap),
        [block],
        scratch=[
            local,
            pltpu.VMEM(serve_rows.shape, jnp.int32),
            pltpu.VMEM((params, serve_rows.shape[1]), jnp.float32),
            pltpu.SemaphoreType.DMA((5,)),
        ],
        cost=400_000,
        far=2,
    )(direction, serve_rows)
    incoming = exchange(outgoing)
    norms = call(
        norms_kernel,
        [(SUBS, LANES)],
        scratch=[
            local,
            local,
            local,
            pltpu.VMEM(precond.shape, jnp.float32),
            pltpu.SemaphoreType.DMA((4,)),
        ],
        cost=2_000_000,
        far=4,
    )(direction, residual, cam_damping, precond)
    returned = call(
        functools.partial(track_kernel, cap, params),
        [block],
        scratch=[pltpu.VMEM((SUBS, devices * cap), jnp.float32)],
        cost=2_000_000,
    )(incoming, jacobians, obs_slot, obs_mask, land_damping.reshape(1, -1), norms)
    arrived = exchange(returned)
    solution_new, residual_new, pre_new, norm_block, old_norm = call(
        functools.partial(owner_kernel, cap),
        [direction.shape, direction.shape, direction.shape, (1, LANES), (SUBS, LANES)],
        scratch=[pltpu.VMEM((direction.shape[1] // LANES * SUBS, LANES), jnp.float32)],
        cost=2_000_000,
    )(arrived, serve_rows, direction, residual, solution, cam_damping, precond)
    norm_blocks = lax.all_gather(norm_block, AXES, axis=0, tiled=True)
    direction_new = call(final_kernel, [direction.shape], cost=400_000)(
        norm_blocks, old_norm, direction, pre_new
    )
    return (solution_new, residual_new, direction_new)


def solution(mesh):
    return jax.shard_map(
        on_device,
        mesh=mesh,
        in_specs=(
            P(None, None, None, AXES),
            P(None, AXES),
            P(None, AXES),
            P(None, AXES),
            P(None, AXES),
            P(None, None, AXES),
            P(AXES),
            P(None, AXES),
            P(None, AXES),
            P(AXES, None),
        ),
        out_specs=(P(None, AXES), P(None, AXES), P(None, AXES)),
        check_vma=False,
    )
```

```python
import functools

import jax
import jax.numpy as jnp
from jax import lax
from jax.experimental import pallas as pl
from jax.experimental.pallas import tpu as pltpu
from jax.sharding import PartitionSpec as P

LANES = 128
SUBS = 8
WIDE = 256
AXES = ("track", "ses")


def lane_gather(rows, index):
    return jnp.take_along_axis(rows, index, axis=1, mode="promise_in_bounds")


def spread(row, subs=SUBS):
    return jnp.broadcast_to(row, (subs, row.shape[1]))


def part(value, size):
    return value >> (size.bit_length() - 1) if size & (size - 1) == 0 else lax.div(value, jnp.int32(size))


def rest(value, size):
    return value & (size - 1) if size & (size - 1) == 0 else lax.rem(value, jnp.int32(size))


def iota(shape, dim):
    return lax.broadcasted_iota(jnp.int32, shape, dim)


def each(count, body):
    if count <= 8:
        for j in range(count):
            body(j)
    else:
        lax.fori_loop(0, count, lambda j, c: (body(j), c)[1], 0)


def at_group(j):
    if isinstance(j, int):
        return pl.ds(j * LANES, LANES)
    return pl.ds(pl.multiple_of(j * LANES, LANES), LANES)


def at_rows(j, size=SUBS):
    if isinstance(j, int):
        return pl.ds(j * size, size)
    return pl.ds(pl.multiple_of(j * size, size), size)


def rows_to_blocks(rows, cap, params):
    per = LANES // cap
    lane = iota((per, LANES), 1)
    index = iota((per, LANES), 0) * cap + rest(lane, cap)
    out = jnp.zeros((per, LANES), rows.dtype)
    for k in range(params):
        picked = lane_gather(spread(rows[k : k + 1], per), index)
        out = jnp.where(part(lane, cap) == k, picked, out)
    return out


def blocks_to_rows(blocks, cap, params):
    per = LANES // cap
    lane = iota((SUBS, LANES), 1)
    sub = iota((SUBS, LANES), 0)
    index = jnp.minimum(sub, params - 1) * cap + rest(lane, cap)
    out = jnp.zeros((SUBS, LANES), blocks.dtype)
    for src in range(per):
        picked = lane_gather(spread(blocks[src : src + 1]), index)
        out = jnp.where(part(lane, cap) == src, picked, out)
    return jnp.where(sub < params, out, 0.0)


def split_bf16(value, parts):
    pieces = []
    rest = value
    for p in range(parts):
        piece = rest.astype(jnp.bfloat16)
        pieces.append(piece)
        if p + 1 < parts:
            rest = rest - piece.astype(jnp.float32)
    return pieces


def split_rounded(value, parts):
    return [piece.astype(jnp.float32) for piece in split_bf16(value, parts)]


def apply_precond(precond, vector):
    params = vector.shape[0]
    total = precond[0] * vector[0:1]
    for k in range(1, params):
        total = total + precond[k] * vector[k : k + 1]
    return total


def one_hot(row, width):
    rows = iota((width, row.shape[1]), 0) == spread(row, width)
    return jnp.where(rows, 1.0, 0.0).astype(jnp.bfloat16)


def norms_of(direction, residual, damping, precond):
    params, count = residual.shape
    old = jnp.zeros((params, LANES), jnp.float32)
    curv = jnp.zeros((params, LANES), jnp.float32)
    for h in range(count // LANES):
        at = slice(h * LANES, (h + 1) * LANES)
        res = residual[:, at]
        pre = apply_precond([precond[k, :, at] for k in range(params)], res)
        old = old + res * pre
        dire = direction[0:params, at]
        curv = curv + damping[:, at] * dire * dire
    return jnp.sum(old), jnp.sum(curv)


def serve_kernel(direction_far, served_far, damp_far, rows, direction, served, damp, padded, sems):
    params, count = direction_far.shape
    slab = min(served.shape[1], 4 * LANES)
    highs = count // WIDE
    copies = [
        pltpu.make_async_copy(direction_far, direction, sems.at[0]),
        pltpu.make_async_copy(served_far, served, sems.at[1]),
        pltpu.make_async_copy(damp_far, damp, sems.at[2]),
    ]
    for copy in copies:
        copy.start()
    padded[params:SUBS, :] = jnp.zeros((SUBS - params, count), jnp.float32)
    copies[1].wait()
    one_slab = slab == served.shape[1]

    def places(j):
        row = served[:, at_rows(j, slab)]
        return one_hot(rest(row, WIDE), WIDE), spread(part(row, WIDE))

    first = places(0) if one_slab else None
    copies[2].wait()
    copies[0].wait()
    padded[0:params, :] = direction[...]
    stacked = jnp.concatenate([padded[:, h * WIDE : (h + 1) * WIDE] for h in range(highs)], axis=0)
    stacked = jnp.concatenate(split_bf16(stacked, 3), axis=0)

    def serve(j):
        at_low, high = first if one_slab else places(j)
        found = jnp.dot(stacked, at_low, preferred_element_type=jnp.float32)
        found = found.reshape(3, highs, SUBS, slab)
        pieces = [found[p, 0] for p in range(3)]
        for h in range(1, highs):
            here = high == h
            pieces = [jnp.where(here, found[p, h], pieces[p]) for p in range(3)]
        rows[:, at_rows(j, slab)] = pieces[0] + pieces[1] + pieces[2]

    each(served.shape[1] // slab, serve)


def arrange_kernel(cap, params, rows, outgoing):
    per = LANES // cap

    def body(j):
        outgoing[at_rows(j, per), :] = rows_to_blocks(rows[:, at_group(j)], cap, params)

    each(rows.shape[1] // LANES, body)


def track_kernel(
    cap, params, incoming, jac, slots, mask, damp, direction, residual, damping, precond,
    returned, table,
):
    devices = incoming.shape[0]
    per = LANES // cap
    groups = devices // per
    obs, tracks = slots.shape

    def fill(j):
        table[:, at_group(j)] = blocks_to_rows(incoming[at_rows(j, per), :], cap, params)

    each(groups, fill)

    slot = slots[...]
    owner = part(slot, cap)
    within = rest(slot, cap)
    halves = [slice(t * LANES, (t + 1) * LANES) for t in range(tracks // LANES)]
    low = [rest(slot[:, at], LANES) for at in halves]
    high = [part(slot[:, at], LANES) for at in halves]

    def look(j, camera):
        rows = table[:, at_group(j)]
        out = []
        for k in range(params):
            source = spread(rows[k : k + 1], obs)
            for t in range(len(halves)):
                picked = lane_gather(source, low[t])
                out.append(jnp.where(high[t] == j, picked, camera[len(out)]))
        return tuple(out)

    camera = tuple(jnp.zeros((obs, LANES), jnp.float32) for _ in range(params * len(halves)))
    if groups <= 8:
        for j in range(groups):
            camera = look(j, camera)
    else:
        camera = lax.fori_loop(0, groups, look, camera)
    camera = [
        jnp.concatenate(camera[k * len(halves) : (k + 1) * len(halves)], axis=1)
        for k in range(params)
    ]

    live = mask[...].astype(jnp.float32)
    cam = [[jac[a, k] for k in range(params)] for a in range(2)]
    land = [[jac[a, params + i] for i in range(3)] for a in range(2)]
    projected = []
    for a in range(2):
        total = cam[a][0] * camera[0]
        for k in range(1, params):
            total = total + cam[a][k] * camera[k]
        projected.append(total)
    weighted = [[land[a][i] * live for i in range(3)] for a in range(2)]

    def over_slots(value):
        return jnp.sum(value, axis=0, keepdims=True)

    normal = {}
    for i in range(3):
        for j in range(i, 3):
            entry = over_slots(weighted[0][i] * land[0][j] + weighted[1][i] * land[1][j])
            if i == j:
                entry = entry + damp[...]
            normal[i, j] = entry
            normal[j, i] = entry
    rhs = [over_slots(weighted[0][i] * projected[0] + weighted[1][i] * projected[1]) for i in range(3)]
    cof = [
        [
            normal[(i + 1) % 3, (j + 1) % 3] * normal[(i + 2) % 3, (j + 2) % 3]
            - normal[(i + 1) % 3, (j + 2) % 3] * normal[(i + 2) % 3, (j + 1) % 3]
            for j in range(3)
        ]
        for i in range(3)
    ]
    det = normal[0, 0] * cof[0][0] + normal[0, 1] * cof[0][1] + normal[0, 2] * cof[0][2]
    step = [
        (cof[0][i] * rhs[0] + cof[1][i] * rhs[1] + cof[2][i] * rhs[2]) / det for i in range(3)
    ]
    res = [
        live
        * (projected[a] - (land[a][0] * step[0] + land[a][1] * step[1] + land[a][2] * step[2]))
        for a in range(2)
    ]
    curv = jnp.sum(res[0] * projected[0] + res[1] * projected[1])
    grad = [cam[0][k] * res[0] + cam[1][k] * res[1] for k in range(params)]

    owner_id = iota((devices, tracks), 0)
    within_id = iota((cap, tracks), 0)
    pieces = [split_rounded(grad[k], 2) for k in range(params)]
    owners, values = [], []
    for o in range(obs):
        at_owner = spread(owner[o : o + 1], devices) == owner_id
        owners.append(jnp.where(at_owner, 1.0, 0.0).astype(jnp.bfloat16))
        at_within = spread(within[o : o + 1], cap) == within_id
        values.append(
            [
                jnp.concatenate(
                    [
                        jnp.where(at_within, spread(pieces[k][p][o : o + 1], cap), 0.0)
                        for k in range(params)
                    ],
                    axis=0,
                ).astype(jnp.bfloat16)
                for p in range(2)
            ]
        )
    total = lax.dot_general(
        jnp.concatenate(owners * 2, axis=1),
        jnp.concatenate([values[o][p] for p in range(2) for o in range(obs)], axis=1),
        (((1,), (1,)), ((), ())),
        preferred_element_type=jnp.float32,
    )
    used = params * cap
    spare = (devices, LANES - used)
    old, own_curv = norms_of(direction, residual, damping, precond)
    returned[:, 0:used] = total
    returned[:, used:LANES] = jnp.where(iota(spare, 1) == 0, old, own_curv + curv)


def owner_kernel(
    cap, arrived, served, direction, residual, solution, damping, precond,
    solution_new, residual_new, pre_new, norm_block, old_norm, summed,
):
    params, count = residual.shape
    devices = arrived.shape[0]
    per = LANES // cap
    slab = min(devices // per, 4)
    highs = count // LANES
    wide_highs = count // WIDE

    def body(j, first):
        weights, lows = [[], []], []
        for g in range(slab):
            rows = blocks_to_rows(arrived[at_rows(j * slab + g, per), :], cap, params)
            row = served[:, at_group(j * slab + g)]
            lows.append(one_hot(rest(row, WIDE), WIDE))
            high = spread(part(row, WIDE))
            for p, piece in enumerate(split_rounded(rows, 2)):
                weights[p].append(
                    jnp.concatenate(
                        [jnp.where(high == h, piece, 0.0) for h in range(wide_highs)], axis=0
                    ).astype(jnp.bfloat16)
                )
        total = lax.dot_general(
            jnp.concatenate([jnp.concatenate(weights[p], axis=1) for p in range(2)], axis=0),
            jnp.concatenate(lows, axis=1),
            (((1,), (1,)), ((), ())),
            preferred_element_type=jnp.float32,
        )
        total = total[: wide_highs * SUBS] + total[wide_highs * SUBS :]
        summed[...] = total if first else summed[...] + total

    slabs = devices // per // slab
    body(0, True)
    if slabs > 1:
        lax.fori_loop(1, slabs, lambda j, c: (body(j, False), c)[1], 0)

    totals = jnp.sum(arrived[...], axis=0, keepdims=True)
    old = totals[:, params * cap : params * cap + 1]
    curv = totals[:, params * cap + 1 : params * cap + 2]
    step_size = old / curv
    step = jnp.broadcast_to(step_size, (params, LANES))
    new = jnp.zeros((params, LANES), jnp.float32)
    for h in range(highs):
        at = slice(h * LANES, (h + 1) * LANES)
        dire = direction[0:params, at]
        image = damping[:, at] * dire + summed[h // 2 * SUBS : h // 2 * SUBS + params, h % 2 * LANES : (h % 2 + 1) * LANES]
        solution_new[:, at] = solution[:, at] + step * dire
        res = residual[:, at] - step * image
        residual_new[:, at] = res
        pre = apply_precond([precond[k, :, at] for k in range(params)], res)
        pre_new[:, at] = pre
        new = new + res * pre
    norm_block[...] = jnp.broadcast_to(jnp.sum(new), norm_block.shape)
    old_norm[...] = jnp.broadcast_to(old, old_norm.shape)


def final_kernel(
    norm_blocks, old_norm, direction, pre_new, solution_near, residual_near,
    solution_new, residual_new, direction_new, local, sems,
):
    params, count = pre_new.shape
    cuts = sems.shape[0] - 2
    width = count // cuts
    copies = [
        pltpu.make_async_copy(solution_near, solution_new, sems.at[cuts]),
        pltpu.make_async_copy(residual_near, residual_new, sems.at[cuts + 1]),
    ]
    for copy in copies:
        copy.start()
    new = jnp.sum(norm_blocks[...], axis=0, keepdims=True)
    ratio = jnp.broadcast_to(new / old_norm[0:1, :], (params, LANES))
    for c in range(cuts):
        for h in range(c * width // LANES, (c + 1) * width // LANES):
            at = slice(h * LANES, (h + 1) * LANES)
            local[:, at] = pre_new[:, at] + ratio * direction[0:params, at]
        at = pl.ds(c * width, width)
        copies.append(pltpu.make_async_copy(local.at[:, at], direction_new.at[:, at], sems.at[c]))
        copies[-1].start()
    for copy in copies:
        copy.wait()


def call(kernel, outs, scratch=(), cost=0, far=0, near=(), out=None):
    outs = [o if hasattr(o, "dtype") else jax.ShapeDtypeStruct(o, jnp.float32) for o in outs]
    shapes = [
        pltpu.VMEM(o.shape, o.dtype) if i in near else jax.ShapeDtypeStruct(o.shape, o.dtype)
        for i, o in enumerate(outs)
    ]
    away = pl.BlockSpec(memory_space=pltpu.HBM)
    places = {"in_specs": [away] * far} if far else {}
    if out == "far":
        places["out_specs"] = [away] * len(outs)
    run = pl.pallas_call(
        kernel,
        **places,
        out_shape=shapes[0] if len(shapes) == 1 else shapes,
        scratch_shapes=scratch,
        compiler_params=pltpu.CompilerParams(vmem_limit_bytes=32 * 1024 * 1024),
        cost_estimate=pl.CostEstimate(flops=cost, bytes_accessed=cost, transcendentals=0),
    )
    if not far:
        return run
    return lambda *args: run(*[pltpu.with_memory_space_constraint(a, pltpu.HBM) for a in args])


def exchange(blocks):
    return lax.all_to_all(blocks, AXES, split_axis=0, concat_axis=0, tiled=True)


def on_device(
    jacobians,
    direction,
    residual,
    solution,
    cam_damping,
    precond,
    land_damping,
    obs_slot,
    obs_mask,
    serve_rows,
):
    devices = lax.axis_size("track") * lax.axis_size("ses")
    params = direction.shape[0]
    cap = serve_rows.shape[1] // devices
    block = (devices, LANES)

    damp = land_damping.reshape(1, -1)
    rows, near_direction, near_served, near_damp = call(
        serve_kernel,
        [(SUBS, devices * cap), direction, serve_rows, damp],
        scratch=[
            pltpu.VMEM((SUBS, direction.shape[1]), jnp.float32),
            pltpu.SemaphoreType.DMA((3,)),
        ],
        cost=20_000,
        far=3,
        near=(0, 1, 2, 3),
    )(direction, serve_rows, damp)
    outgoing = call(
        functools.partial(arrange_kernel, cap, params), [block], cost=2_000_000_000, near=(0,)
    )(rows)
    incoming = exchange(outgoing)
    returned = call(
        functools.partial(track_kernel, cap, params),
        [block],
        scratch=[pltpu.VMEM((SUBS, devices * cap), jnp.float32)],
        cost=2_000_000,
    )(
        incoming, jacobians, obs_slot, obs_mask, near_damp,
        near_direction, residual, cam_damping, precond,
    )
    arrived = exchange(returned)
    solution_new, residual_new, pre_new, norm_block, old_norm = call(
        functools.partial(owner_kernel, cap),
        [direction.shape, direction.shape, direction.shape, block, (SUBS, LANES)],
        scratch=[pltpu.VMEM((direction.shape[1] // WIDE * SUBS, WIDE), jnp.float32)],
        cost=2_000_000,
        near=(0, 1, 2),
    )(
        arrived, near_served, near_direction, residual, solution, cam_damping, precond
    )
    norm_blocks = exchange(norm_block)
    return tuple(
        call(
            final_kernel,
            [direction.shape] * 3,
            scratch=[pltpu.VMEM(direction.shape, jnp.float32), pltpu.SemaphoreType.DMA((4,))],
            cost=400_000,
            out="far",
        )(norm_blocks, old_norm, near_direction, pre_new, solution_new, residual_new)
    )


def solution(mesh):
    return jax.shard_map(
        on_device,
        mesh=mesh,
        in_specs=(
            P(None, None, None, AXES),
            P(None, AXES),
            P(None, AXES),
            P(None, AXES),
            P(None, AXES),
            P(None, None, AXES),
            P(AXES),
            P(None, AXES),
            P(None, AXES),
            P(AXES, None),
        ),
        out_specs=(P(None, AXES), P(None, AXES), P(None, AXES)),
        check_vma=False,
    )
```
